32 devices in a mesh: parts: 2 (over x), grp: 2 (over core), pan: 8 (over z, y).
Axes of the slice: x: 2, y: 2, z: 4, core: 2. Of those that a mesh axis runs over, the one named last changes fastest.
Arguments:
- surface_field: float32 [1536, 2, 16, 128], P(('parts', 'grp', 'pan')), parts along dimension 0, may hold values from -6 to 6
- positions: bfloat16 [1536, 3, 128], P(('parts', 'grp', 'pan')), parts along dimension 0, may hold values from 0 to 1
- quad_weight: float32 [1536, 128], P(('parts', 'grp', 'pan')), parts along dimension 0, may hold values from 0.2 to 1
- octree_order: int32 [32, 48], P(('parts', 'grp', 'pan')), parts along dimension 0, may hold values from 0 to 47, each once within a row
- near_target: int32 [32, 144], P('parts'), parts along dimension 0, may hold values from 0 to 47
- near_source: int32 [32, 144], P('parts'), parts along dimension 0, may hold values from 0 to 143
- near_count: int32 [32], P('parts'), parts along dimension 0, may hold values from 36 to 144, as said below
- compress: bfloat16 [1536, 128, 128], P(('parts', 'grp', 'pan')), parts along dimension 0, may hold values from -0.375 to 0.375
- expand: bfloat16 [1536, 64, 256], P(('parts', 'grp', 'pan')), parts along dimension 0, may hold values from -0.5 to 0.5
- mixing: bfloat16 [4, 768, 2, 2, 64, 128], P(None, ('parts', 'grp', 'pan')), parts along dimension 1, may hold values from -0.375 to 0.375
Outputs:
- operator_image: float32 [1536, 2, 16, 128], P(('parts', 'grp', 'pan')), parts along dimension 0
The draws below stay inside these ranges and needn't reach their ends.
There are 2 independent parts, one for each index of `parts`. The reference program is written for one: setup_inputs(seed, part) draws one part's arguments, and reference() takes and returns one part's arrays. A program takes and returns all parts, laid end to end along the dimension named above; each array names one. Nothing has to cross between parts.
Inputs may be any that keep to these rules, and one draw needn't show every extreme that they name: `octree_order`: each row is a permutation of the panel slots. `near_count`: pair slots from the count on are ignored; some device has exactly 144 live pairs.
All inputs are finite; a program needn't handle non-finite values.
Results may differ from the reference program's by a relative error of at most 0.0048.
Values may be sent and summed in bfloat16 or wider, within the bound.
A program may use at most 64 MiB of HBM per device.

```python
import math
import jax
import jax.numpy as jnp
from jax import lax

P_DEV = 48
B = 128
K = 64
RHS = 16
LEVELS = 4
NDEV = 16
PANELS = 768
NEAR_MAX = 144
N_PAN = 8


def draw_near_count(key, part):
    key = jax.random.fold_in(key, 11)
    key_base, key_heavy, key_top, key_low = jax.random.split(key, 4)
    base_counts = jax.random.randint(key_base, (NDEV,), NEAR_MAX // 4, NEAR_MAX // 2 + 1)
    heavy_mask = jax.random.randint(key_heavy, (NDEV,), 0, 8) == 0
    top_device = jax.random.randint(key_top, (), 0, NDEV)
    low_device = (top_device + 1 + jax.random.randint(key_low, (), 0, NDEV - 1)) % NDEV
    device_ids = jnp.arange(NDEV)
    counts = jnp.where(heavy_mask | (device_ids == top_device), NEAR_MAX, base_counts)
    counts = jnp.where(device_ids == low_device, NEAR_MAX // 4, counts)
    return counts.astype(jnp.int32)


def set_ends(entries, own_key, low, largest):
    longest = entries.shape.index(max(entries.shape))
    spots = []
    for shift in (0, 1):
        where = [jax.random.randint(jax.random.fold_in(own_key, axis), (), 0, length) for axis, length in enumerate(entries.shape)]
        where[longest] = (where[longest] + shift) % entries.shape[longest]
        spots.append(tuple(where))
    return entries.at[spots[0]].set(low).at[spots[1]].set(largest)


def levels(key, shape, shards, least, largest):
    loudness = 1.0
    for dim, blocks in shards:
        draws = jax.random.uniform(jax.random.fold_in(jax.random.fold_in(key, 6), dim), (blocks,), jnp.float32, least / len(shards), largest / len(shards))
        loudness = loudness * jnp.repeat(jnp.exp(draws), shape[dim] // blocks).reshape((-1,) + (1,) * (len(shape) - 1 - dim))
    return loudness


def normal_values(own_key, shape, deviation, most, pieces=(), kind=jnp.bfloat16):
    array = jax.random.normal(own_key, shape, jnp.float32) * deviation
    if len(pieces) > 0:
        array = levels(own_key, shape, pieces, -0.22, 0.18) * array
    return jnp.clip(array, min=-most, max=most).astype(kind)


def setup_inputs(seed: int = 0, part: int = 0) -> dict:
    arg_keys = jax.random.split(jax.random.key(seed), 11)
    part_splits = jax.random.split(jax.random.fold_in(arg_keys[10], part), 11)
    return {
        "surface_field": normal_values(part_splits[0], (PANELS, 2, RHS, B), 1.0, 6.0, ((0, 16),), jnp.float32),
        "positions": jnp.clip(1.0 * jax.random.uniform(part_splits[1], (PANELS, 3, B), jnp.float32) ** levels(part_splits[1], (PANELS, 3, B), ((0, 16),), -0.2, 0.2), 0.0, 1.0).astype(jnp.bfloat16),
        "quad_weight": jnp.clip(jnp.exp(math.log(1.0) - 1.609438 * jax.random.uniform(part_splits[2], (PANELS, B), jnp.float32) ** levels(part_splits[2], (PANELS, B), ((0, 16),), -0.2, 0.2)), 0.2, 1.0),
        "octree_order": jax.vmap(lambda own: jax.random.permutation(own, P_DEV))(jax.random.split(part_splits[3], NDEV)).reshape((NDEV, P_DEV)).astype(jnp.int32),
        "near_target": set_ends(jax.random.randint(part_splits[4], (NDEV, NEAR_MAX), 0, P_DEV), jax.random.fold_in(part_splits[4], 1), 0, P_DEV - 1).astype(jnp.int32),
        "near_source": set_ends(jax.random.randint(part_splits[5], (NDEV, NEAR_MAX), 0, 3 * P_DEV), jax.random.fold_in(part_splits[5], 1), 0, (3 * P_DEV) - 1).astype(jnp.int32),
        "near_count": draw_near_count(jax.random.fold_in(jax.random.fold_in(arg_keys[10], part), 71), part),
        "compress": normal_values(part_splits[7], (PANELS, B, 2 * K), (2 * B) ** -0.5, 0.375, ((0, 16),)),
        "expand": normal_values(part_splits[8], (PANELS, K, 2 * B), (2 * K) ** -0.5, 0.5, ((0, 16),)),
        "mixing": normal_values(part_splits[9], (LEVELS, PANELS // 2, 2, 2, K, 2 * K), (4 * K) ** -0.5, 0.375, ((1, 16),)),
    }


wavenumber = 6.0
softening = 0.05

def pair_kernels(src_points, tgt_points):
    offsets = src_points.astype(jnp.float32)[:, :, :, None] - tgt_points.astype(jnp.float32)[:, :, None, :]
    distance = jnp.sqrt(lax.optimization_barrier(jnp.sum(offsets * offsets, axis=1)) + softening * softening)
    amplitude = 1.0 / (4.0 * math.pi * distance)
    kernel_tiles = jnp.concatenate([amplitude * jnp.cos(wavenumber * distance), amplitude * jnp.sin(wavenumber * distance)], -1)
    return kernel_tiles.astype(jnp.bfloat16)

def complex_apply(values, kernel_tiles):
    products = jnp.einsum('gcrb,gbm->gcrm', values.astype(jnp.float32), kernel_tiles.astype(jnp.float32))
    tile_width = kernel_tiles.shape[1]
    real_out = products[:, 0, :, :tile_width] - products[:, 1, :, tile_width:]
    imag_out = products[:, 0, :, tile_width:] + products[:, 1, :, :tile_width]
    return jnp.stack([real_out, imag_out], 1)

def reference(surface_field, positions, quad_weight, octree_order, near_target, near_source, near_count, compress, expand, mixing):
    octree_rows = (jnp.arange(NDEV, dtype=jnp.int32)[:, None] * P_DEV + octree_order).reshape(-1).astype(jnp.int32)
    weighted = (surface_field * quad_weight[:, None, None, :]).astype(jnp.bfloat16)
    sources = weighted[octree_rows]
    points = positions[octree_rows]
    padded_src = jnp.pad(sources, ((P_DEV, P_DEV), (0, 0), (0, 0), (0, 0)))
    padded_pts = jnp.pad(points, ((P_DEV, P_DEV), (0, 0), (0, 0)))

    def device_near(device):
        start = (device * P_DEV).astype(jnp.int32)
        win_src = lax.dynamic_slice_in_dim(padded_src, start, 3 * P_DEV, 0)
        win_pts = lax.dynamic_slice_in_dim(padded_pts, start, 3 * P_DEV, 0)
        tgt_pts = lax.dynamic_slice_in_dim(points, start, P_DEV, 0)
        tgt_rows = near_target[device]
        src_rows = near_source[device]
        live_mask = (jnp.arange(NEAR_MAX, dtype=jnp.int32) < near_count[device]).astype(jnp.float32)
        kernel_tiles = pair_kernels(win_pts[src_rows], tgt_pts[tgt_rows])
        pair_terms = complex_apply(win_src[src_rows], kernel_tiles) * live_mask[:, None, None, None]
        return jnp.zeros((P_DEV, 2, RHS, B), jnp.float32).at[tgt_rows].add(pair_terms)
    near_part = lax.map(device_near, jnp.arange(NDEV, dtype=jnp.int32)).reshape(PANELS, 2, RHS, B)
    spectrum = jnp.einsum('pcrb,pbm->pcrm', sources.astype(jnp.float32), compress.astype(jnp.float32))
    coeffs = jnp.concatenate([spectrum[:, 0, :, :K] - spectrum[:, 1, :, K:], spectrum[:, 0, :, K:] + spectrum[:, 1, :, :K]], -1).astype(jnp.bfloat16)
    half_slots = P_DEV // 2
    for level in range(LEVELS):
        distance = N_PAN if level == 0 else N_PAN // 2 ** level
        blocks = coeffs.reshape(NDEV // (2 * distance), 2, distance, 2, half_slots, RHS, 2 * K)
        stacked = jnp.transpose(blocks, (0, 3, 2, 1, 4, 5, 6)).reshape(NDEV, 2, half_slots, RHS, 2 * K).astype(jnp.float32)
        weights = mixing[level].reshape(NDEV, half_slots, 2, 2, K, 2 * K).astype(jnp.float32)
        real_part = jnp.einsum('gihrk,ghoikm->gohrm', stacked[..., :K], weights)
        imag_part = jnp.einsum('gihrk,ghoikm->gohrm', stacked[..., K:], weights)
        mixed_out = jnp.concatenate([real_part[..., :K] - imag_part[..., K:], real_part[..., K:] + imag_part[..., :K]], -1)
        coeffs = mixed_out.reshape(PANELS, RHS, 2 * K).astype(jnp.bfloat16)
    real_part = jnp.einsum('prk,pkm->prm', coeffs[..., :K].astype(jnp.float32), expand.astype(jnp.float32))
    imag_part = jnp.einsum('prk,pkm->prm', coeffs[..., K:].astype(jnp.float32), expand.astype(jnp.float32))
    far_part = jnp.stack([real_part[..., :B] - imag_part[..., B:], real_part[..., B:] + imag_part[..., :B]], 1)
    summed = near_part + far_part
    return jnp.zeros_like(summed).at[octree_rows].set(summed)
```

```python
import functools
import math

import jax
import jax.numpy as jnp
from jax import lax
from jax.experimental import pallas as pl
from jax.experimental.pallas import tpu as pltpu
from jax.sharding import PartitionSpec as P

wavenumber = 6.0
softening = 0.05

SIN = (3.14159264, -5.16771008, 2.55007752, -0.59829129, 0.07765766)
COS = (0.99999995, -4.93479283, 4.05841135, -1.33187657, 0.21968961)
PER_TURN = wavenumber / (2.0 * math.pi)
AMPLITUDE = PER_TURN / (4.0 * math.pi)
FEATURES = 16


def loop(count, body, width):
    width = math.gcd(count, width)

    def step(index, carry):
        for inner in range(width):
            body(index * width + inner)
        return carry

    lax.fori_loop(0, count // width, step, 0)


def poly(values, coeffs):
    total = coeffs[-1]
    for coeff in coeffs[-2::-1]:
        total = total * values + coeff
    return total


def pieces(values):
    parts = []
    for _ in range(3):
        part = values.astype(jnp.bfloat16).astype(jnp.float32)
        parts.append(part)
        values = values - part
    return parts


def kernel(
    ids,
    field,
    weight,
    positions,
    compress_hbm,
    expand_hbm,
    mixing_hbm,
    out,
    compress,
    expand,
    mixing,
    win,
    pts_raw,
    pts,
    src_feat,
    tgt_feat,
    tiles,
    coeffs,
    landed,
    far,
    running,
    load_sem,
    send_sem,
    recv_sem,
    *,
    pairs,
    spread,
    devices,
):
    panels = field.shape[0]
    rows = field.shape[1]
    half_rows = rows // 2
    width = field.shape[2]
    half = panels // 2
    levels = mixing.shape[0]
    rank2 = compress.shape[2]
    rank = rank2 // 2
    at_src, at_tgt, at_keep = 0, pairs, 2 * pairs
    at_order = 3 * pairs
    at_inv, at_end = at_order + panels, at_order + 2 * panels

    group = lax.axis_index("grp")
    slot = lax.axis_index("pan")
    device = group * spread + slot
    has_prev = device > 0
    has_next = device < devices - 1
    prev = lax.rem(device + devices - 1, devices)
    next_ = lax.rem(device + 1, devices)

    def place(number):
        return {"grp": number // spread, "pan": lax.rem(number, spread)}

    loads = [
        pltpu.make_async_copy(compress_hbm, compress, load_sem.at[0]),
        pltpu.make_async_copy(expand_hbm, expand, load_sem.at[1]),
    ] + [
        pltpu.make_async_copy(mixing_hbm.at[level], mixing.at[level], load_sem.at[2 + level])
        for level in range(levels)
    ]
    for load in loads:
        load.start()

    top_bit = spread.bit_length() - 1
    bits, partners = [], []
    for level in range(levels):
        if level == 0:
            bit = group
            partners.append({"grp": 1 - group, "pan": slot})
        else:
            stride = 1 << (top_bit - level)
            bit = lax.rem(slot // stride, 2)
            partners.append({"grp": group, "pan": slot + stride - 2 * stride * bit})
        bits.append(bit)

    barrier = pltpu.get_barrier_semaphore()
    for other in partners:
        pl.semaphore_signal(barrier, inc=1, device_id=other, device_id_type=pl.DeviceIdType.MESH)

    @pl.when(has_prev)
    def _():
        pl.semaphore_signal(
            barrier, inc=1, device_id=place(prev), device_id_type=pl.DeviceIdType.MESH
        )

    @pl.when(has_next)
    def _():
        pl.semaphore_signal(
            barrier, inc=1, device_id=place(next_), device_id_type=pl.DeviceIdType.MESH
        )

    def gather_points(panel):
        xyz = positions[ids[at_order + panel]].astype(jnp.float32)
        for axis in range(3):
            pts_raw[pl.ds(axis * panels + panel, 1), :] = xyz[axis : axis + 1, :]

    loop(panels, gather_points, 8)
    pts[3 * panels : 6 * panels] = pts_raw[...].astype(jnp.bfloat16)

    def third(ref, window):
        return ref.at[pl.ds(window * (ref.shape[0] // 3), ref.shape[0] // 3)]

    def window_copies(ref, base):
        to_next = pltpu.make_async_remote_copy(
            src_ref=third(ref, 1),
            dst_ref=third(ref, 0),
            send_sem=send_sem.at[base],
            recv_sem=recv_sem.at[base],
            device_id=place(next_),
            device_id_type=pl.DeviceIdType.MESH,
        )
        to_prev = pltpu.make_async_remote_copy(
            src_ref=third(ref, 1),
            dst_ref=third(ref, 2),
            send_sem=send_sem.at[base + 1],
            recv_sem=recv_sem.at[base + 1],
            device_id=place(prev),
            device_id_type=pl.DeviceIdType.MESH,
        )
        return to_next, to_prev

    def start_window(copies):
        @pl.when(has_next)
        def _():
            copies[0].start()

        @pl.when(has_prev)
        def _():
            copies[1].start()

    def wait_window(copies, ref):
        @pl.when(has_prev)
        def _():
            copies[0].wait_recv()
            copies[1].wait_send()

        @pl.when(has_next)
        def _():
            copies[1].wait_recv()
            copies[0].wait_send()

        @pl.when(jnp.logical_not(has_prev))
        def _():
            third(ref, 0)[...] = jnp.zeros((ref.shape[0] // 3,) + ref.shape[1:], ref.dtype)

        @pl.when(jnp.logical_not(has_next))
        def _():
            third(ref, 2)[...] = jnp.zeros((ref.shape[0] // 3,) + ref.shape[1:], ref.dtype)

    pl.semaphore_wait(
        barrier, levels + has_prev.astype(jnp.int32) + has_next.astype(jnp.int32)
    )
    point_copies = window_copies(pts, 0)
    start_window(point_copies)

    def gather_sources(panel):
        row = ids[at_order + panel]
        win[panels + panel] = (field[row] * weight[pl.ds(row, 1), :]).astype(jnp.bfloat16)

    loop(panels, gather_sources, 8)
    source_copies = window_copies(win, 2)

    lane = lax.broadcasted_iota(jnp.int32, (half_rows, rank2), 1)
    low_lanes = lane < rank
    sign = jnp.where(low_lanes, -1.0, 1.0)

    def fold(product):
        return product[:half_rows] + sign * pltpu.roll(product[half_rows:], rank, 1)

    loads[0].wait()

    def compress_panel(panel):
        product = jnp.dot(win[panels + panel], compress[panel], preferred_element_type=jnp.float32)
        coeffs[0, panel] = fold(product).astype(jnp.bfloat16)

    loop(panels, compress_panel, 8)

    def level_copy(level):
        return pltpu.make_async_remote_copy(
            src_ref=coeffs.at[level, pl.ds((1 - bits[level]) * half, half)],
            dst_ref=landed.at[level],
            send_sem=send_sem.at[4 + level],
            recv_sem=recv_sem.at[4 + level],
            device_id=partners[level],
            device_id_type=pl.DeviceIdType.MESH,
        )

    level_copies = [level_copy(0)]
    level_copies[0].start()
    start_window(source_copies)

    ones = jnp.ones((panels, width), jnp.float32)

    def source_features(window):
        xyz = third(pts, window)[...].astype(jnp.float32)
        square = jnp.full((panels, width), softening * softening, jnp.float32)
        stack = []
        for axis in range(3):
            x = xyz[axis * panels : (axis + 1) * panels]
            square = square + x * x
            stack += [x] * 3
        stack += pieces(square * (PER_TURN * PER_TURN)) + [ones] * 3 + [ones * 0.0]
        for row, values in enumerate(stack):
            src_feat[pl.ds(window * panels, panels), row, :] = values

    def target_features():
        xyz = third(pts, 1)[...].astype(jnp.float32)
        square = jnp.zeros((panels, width), jnp.float32)
        stack = []
        for axis in range(3):
            x = xyz[axis * panels : (axis + 1) * panels]
            square = square + x * x
            stack += pieces(x * (-2.0 * PER_TURN * PER_TURN))
        stack += [ones] * 3 + pieces(square * (PER_TURN * PER_TURN)) + [ones * 0.0]
        for row, values in enumerate(stack):
            tgt_feat[:, row, :] = values

    target_features()
    source_features(1)
    wait_window(point_copies, pts)
    source_features(0)
    source_features(2)

    def make_tile(pair):
        source = src_feat[ids[at_src + pair]].astype(jnp.bfloat16)
        target = tgt_feat[ids[at_tgt + pair]].astype(jnp.bfloat16)
        squared = lax.dot_general(
            source, target, (((0,), (0,)), ((), ())), preferred_element_type=jnp.float32
        )
        inverse = lax.rsqrt(squared)
        turns = squared * inverse
        part = turns - jnp.round(turns)
        square = part * part
        half_sin = part * poly(square, [math.sqrt(2.0 * AMPLITUDE) * c for c in SIN])
        half_cos = poly(square, [math.sqrt(2.0 * AMPLITUDE) * c for c in COS])
        scaled = inverse * half_sin
        tiles[pair, :, :width] = (AMPLITUDE * inverse - scaled * half_sin).astype(jnp.bfloat16)
        tiles[pair, :, width:] = (scaled * half_cos).astype(jnp.bfloat16)

    share = pairs // levels

    def mix_level(level):
        bit = bits[level]

        def mix_slot(index):
            kept = coeffs[level, bit * half + index].astype(jnp.float32)
            other = landed[level, index].astype(jnp.float32)
            low = jnp.where(bit == 1, other, kept)
            high = jnp.where(bit == 1, kept, other)
            real = jnp.where(low_lanes, low, pltpu.roll(high, rank, 1))
            imag = jnp.where(low_lanes, pltpu.roll(low, rank, 1), high)
            stacked = jnp.concatenate([real, imag], 0).astype(jnp.bfloat16)
            for side in range(2):
                product = jnp.dot(
                    stacked, mixing[level, index, side], preferred_element_type=jnp.float32
                )
                coeffs[level + 1, side * half + index] = fold(product).astype(jnp.bfloat16)

        loop(half, mix_slot, 8)

    for level in range(levels):
        first = level * share
        last = pairs if level == levels - 1 else first + share
        loop(last - first, lambda k, first=first: make_tile(first + k), 2)
        loads[2 + level].wait()
        level_copies[level].wait()
        mix_level(level)
        if level + 1 < levels:
            level_copies.append(level_copy(level + 1))
            level_copies[level + 1].start()

    loads[1].wait()

    def expand_panel(panel):
        values = coeffs[levels, panel].astype(jnp.float32)
        stacked = jnp.concatenate([values, pltpu.roll(values, rank, 1)], 0)[:, :rank]
        far[panel] = jnp.dot(
            stacked.astype(jnp.bfloat16), expand[panel], preferred_element_type=jnp.float32
        )

    loop(panels, expand_panel, 8)

    wait_window(source_copies, win)

    running[0] = jnp.zeros(running.shape[1:], jnp.float32)
    group_size = math.gcd(pairs, 4)

    def sum_pairs(index, total):
        for inner in range(group_size):
            pair = index * group_size + inner
            product = jnp.dot(
                win[ids[at_src + pair]],
                tiles[pair],
                preferred_element_type=jnp.float32,
            )
            total = total * ids[at_keep + pair].astype(jnp.float32) + product
            running[1 + pair] = total
        return total

    lax.fori_loop(
        0, pairs // group_size, sum_pairs, jnp.zeros(running.shape[1:], jnp.float32)
    )

    def write_panel(panel):
        total = far[ids[at_inv + panel]] + running[ids[at_end + panel]]
        out[panel, :half_rows] = total[:half_rows, :width] - total[half_rows:, width:]
        out[panel, half_rows:] = total[:half_rows, width:] + total[half_rows:, :width]

    loop(panels, write_panel, 8)


def pair_ids(order, target, source, count):
    panels, pairs = order.shape[0], target.shape[0]
    slots = jnp.arange(pairs, dtype=jnp.int32)
    target = jnp.where(slots < count, target, panels)
    key = target * pairs + slots
    rank = jnp.sum((key[None, :] < key[:, None]).astype(jnp.int32), 1)
    hit = rank[None, :] == slots[:, None]
    both = jnp.sum(jnp.where(hit, (target * (4 * panels) + source)[None, :], 0), 1)
    by_target, by_source = both // (4 * panels), both % (4 * panels)
    keep = jnp.concatenate(
        [jnp.zeros((1,), jnp.int32), (by_target[1:] == by_target[:-1]).astype(jnp.int32)]
    )
    rows = jnp.arange(panels, dtype=jnp.int32)
    inverse = jnp.sum(jnp.where(order[None, :] == rows[:, None], rows[None, :], 0), 1)
    up_to = jnp.sum((target[None, :] <= inverse[:, None]).astype(jnp.int32), 1)
    own = jnp.any(target[None, :] == inverse[:, None], 1)
    end = jnp.where(own, up_to, 0)
    return jnp.concatenate(
        [by_source, jnp.minimum(by_target, panels - 1), keep, order, inverse, end]
    )


def on_device(
    surface_field,
    positions,
    quad_weight,
    octree_order,
    near_target,
    near_source,
    near_count,
    compress,
    expand,
    mixing,
):
    panels, _, rhs, width = surface_field.shape
    levels, half = mixing.shape[:2]
    pairs = near_target.shape[1]
    rank2 = compress.shape[2]
    spread = lax.axis_size("pan")
    devices = spread * lax.axis_size("grp")
    device = lax.axis_index("grp") * spread + lax.axis_index("pan")
    ids = pair_ids(octree_order[0], near_target[device], near_source[device], near_count[device])
    rows = 2 * rhs
    vmem = pl.BlockSpec(memory_space=pltpu.VMEM)
    hbm = pl.BlockSpec(memory_space=pl.ANY)
    result = pl.pallas_call(
        functools.partial(kernel, pairs=pairs, spread=spread, devices=devices),
        out_shape=jax.ShapeDtypeStruct((panels, rows, width), jnp.float32),
        in_specs=[pl.BlockSpec(memory_space=pltpu.SMEM), vmem, vmem, vmem, hbm, hbm, hbm],
        out_specs=vmem,
        scratch_shapes=[
            pltpu.VMEM(compress.shape, jnp.bfloat16),
            pltpu.VMEM(expand.shape, jnp.bfloat16),
            pltpu.VMEM((levels, half, 2, rank2, rank2), jnp.bfloat16),
            pltpu.VMEM((3 * panels, rows, width), jnp.bfloat16),
            pltpu.VMEM((3 * panels, width), jnp.float32),
            pltpu.VMEM((9 * panels, width), jnp.bfloat16),
            pltpu.VMEM((3 * panels, FEATURES, width), jnp.float32),
            pltpu.VMEM((panels, FEATURES, width), jnp.float32),
            pltpu.VMEM((pairs, width, 2 * width), jnp.bfloat16),
            pltpu.VMEM((levels + 1, panels, rhs, rank2), jnp.bfloat16),
            pltpu.VMEM((levels, half, rhs, rank2), jnp.bfloat16),
            pltpu.VMEM((panels, rows, 2 * width), jnp.float32),
            pltpu.VMEM((pairs + 1, rows, 2 * width), jnp.float32),
            pltpu.SemaphoreType.DMA((2 + levels,)),
            pltpu.SemaphoreType.DMA((4 + levels,)),
            pltpu.SemaphoreType.DMA((4 + levels,)),
        ],
        compiler_params=pltpu.CompilerParams(
            collective_id=0, has_side_effects=True, vmem_limit_bytes=56 * 1024 * 1024
        ),
    )(
        ids,
        surface_field.reshape(panels, rows, width),
        quad_weight,
        positions,
        compress,
        expand,
        mixing.reshape(levels, half, 2, rank2, rank2),
    )
    return result.reshape(panels, 2, rhs, width)


def solution(mesh):
    placed = (
        P(("parts", "grp", "pan"), None, None, None),
        P(("parts", "grp", "pan"), None, None),
        P(("parts", "grp", "pan"), None),
        P(("parts", "grp", "pan"), None),
        P("parts", None),
        P("parts", None),
        P("parts"),
        P(("parts", "grp", "pan"), None, None),
        P(("parts", "grp", "pan"), None, None),
        P(None, ("parts", "grp", "pan"), None, None, None, None),
    )
    return jax.shard_map(
        on_device,
        mesh=mesh,
        in_specs=placed,
        out_specs=P(("parts", "grp", "pan"), None, None, None),
        check_vma=False,
    )
```

```python
import functools
import math

import jax
import jax.numpy as jnp
from jax import lax
from jax.experimental import pallas as pl
from jax.experimental.pallas import tpu as pltpu
from jax.sharding import PartitionSpec as P

wavenumber = 6.0
softening = 0.05

SIN = (3.14159264, -5.16771008, 2.55007752, -0.59829129, 0.07765766)
COS = (0.99999995, -4.93479283, 4.05841135, -1.33187657, 0.21968961)
PER_TURN = wavenumber / (2.0 * math.pi)
AMPLITUDE = PER_TURN / (4.0 * math.pi)
FEATURES = 16


def loop(count, load, compute, store, width):
    width = math.gcd(count, width)

    def step(index, carry):
        numbers = [index * width + inner for inner in range(width)]
        values = [load(number) for number in numbers]
        results = [compute(*value) for value in values]
        for number, result in zip(numbers, results):
            store(number, result)
        return carry

    lax.fori_loop(0, count // width, step, 0)


def poly(values, coeffs):
    total = coeffs[-1]
    for coeff in coeffs[-2::-1]:
        total = total * values + coeff
    return total


def pieces(values):
    parts = []
    for _ in range(3):
        part = values.astype(jnp.bfloat16).astype(jnp.float32)
        parts.append(part)
        values = values - part
    return parts


def kernel(
    order_hbm,
    near_target_hbm,
    near_source_hbm,
    near_count_hbm,
    field_hbm,
    weight_hbm,
    positions_hbm,
    compress_hbm,
    expand_hbm,
    mixing_hbm,
    out_hbm,
    order,
    order_vec,
    near_target,
    near_source,
    near_count,
    field,
    weight,
    positions,
    out,
    compress,
    expand,
    mixing,
    win,
    pts_input,
    pts_raw,
    pts,
    src_feat,
    tgt_feat,
    tiles,
    coeffs,
    landed,
    far,
    running,
    ids_vec,
    ids,
    load_sem,
    send_sem,
    recv_sem,
    *,
    pairs,
    spread,
    devices,
):
    panels = field.shape[0]
    rows = field.shape[1]
    half_rows = rows // 2
    width = field.shape[2]
    half = panels // 2
    levels = mixing.shape[0]
    rank2 = compress.shape[2]
    rank = rank2 // 2

    group = lax.axis_index("grp")
    slot = lax.axis_index("pan")
    device = group * spread + slot
    has_prev = device > 0
    has_next = device < devices - 1
    prev = lax.rem(device + devices - 1, devices)
    next_ = lax.rem(device + 1, devices)

    odd = lax.rem(device, 2)
    has_before, has_after = device > 1, device < devices - 2
    before = lax.rem(device + devices - 2, devices)
    after = lax.rem(device + 2, devices)
    passes = jnp.where(odd == 1, device - 2 >= 0, device + 2 < devices)
    gets = jnp.where(odd == 1, device + 2 < devices, device - 2 >= 0)
    pass_to = jnp.where(odd == 1, before, after)

    def place(number):
        return {"grp": number // spread, "pan": lax.rem(number, spread)}

    loads = [
        pltpu.make_async_copy(compress_hbm, compress, load_sem.at[0]),
        pltpu.make_async_copy(expand_hbm, expand, load_sem.at[1]),
    ] + [
        pltpu.make_async_copy(mixing_hbm.at[level], mixing.at[level], load_sem.at[2 + level])
        for level in range(levels)
    ]
    small = [
        pltpu.make_async_copy(source, target, load_sem.at[3 + levels + number])
        for number, (source, target) in enumerate(
            [
                (order_hbm, order),
                (positions_hbm, positions),
                (weight_hbm, weight),
                (field_hbm, field),
                (order_hbm, order_vec),
                (near_target_hbm, near_target),
                (near_source_hbm, near_source),
                (near_count_hbm, near_count),
            ]
        )
    ]
    for load in small + loads:
        load.start()

    top_bit = spread.bit_length() - 1
    bits, partners = [], []
    for level in range(levels):
        if level == 0:
            bit = group
            partners.append({"grp": 1 - group, "pan": slot})
        else:
            stride = 1 << (top_bit - level)
            bit = lax.rem(slot // stride, 2)
            partners.append({"grp": group, "pan": slot + stride - 2 * stride * bit})
        bits.append(bit)

    barrier = pltpu.get_barrier_semaphore()
    for other in partners:
        pl.semaphore_signal(barrier, inc=1, device_id=other, device_id_type=pl.DeviceIdType.MESH)

    @pl.when(has_prev)
    def _():
        pl.semaphore_signal(
            barrier, inc=1, device_id=place(prev), device_id_type=pl.DeviceIdType.MESH
        )

    @pl.when(has_next)
    def _():
        pl.semaphore_signal(
            barrier, inc=1, device_id=place(next_), device_id_type=pl.DeviceIdType.MESH
        )

    small[0].wait()
    small[1].wait()
    pts_input[...] = positions[...].astype(jnp.float32)

    def load_panel(panel):
        row = order[0, panel]
        return [pts_input[pl.ds(axis * panels + row, 1), :] for axis in range(3)]

    def store_panel(panel, xyz):
        for axis in range(3):
            pts_raw[pl.ds(axis * panels + panel, 1), :] = xyz[axis]

    loop(panels, load_panel, lambda *xyz: xyz, store_panel, 16)
    pts[3 * panels : 6 * panels] = pts_raw[...].astype(jnp.bfloat16)

    def third(ref, window):
        return ref.at[pl.ds(window * (ref.shape[0] // 3), ref.shape[0] // 3)]

    def window_copies(ref, base):
        to_next = pltpu.make_async_remote_copy(
            src_ref=third(ref, 1),
            dst_ref=third(ref, 0),
            send_sem=send_sem.at[base],
            recv_sem=recv_sem.at[base],
            device_id=place(next_),
            device_id_type=pl.DeviceIdType.MESH,
        )
        to_prev = pltpu.make_async_remote_copy(
            src_ref=third(ref, 1),
            dst_ref=third(ref, 2),
            send_sem=send_sem.at[base + 1],
            recv_sem=recv_sem.at[base + 1],
            device_id=place(prev),
            device_id_type=pl.DeviceIdType.MESH,
        )
        return to_next, to_prev

    def start_window(copies):
        @pl.when(has_next)
        def _():
            copies[0].start()

        @pl.when(has_prev)
        def _():
            copies[1].start()

    def wait_window(copies, ref):
        @pl.when(has_prev)
        def _():
            copies[0].wait_recv()
            copies[1].wait_send()

        @pl.when(has_next)
        def _():
            copies[1].wait_recv()
            copies[0].wait_send()

        @pl.when(jnp.logical_not(has_prev))
        def _():
            third(ref, 0)[...] = jnp.zeros((ref.shape[0] // 3,) + ref.shape[1:], ref.dtype)

        @pl.when(jnp.logical_not(has_next))
        def _():
            third(ref, 2)[...] = jnp.zeros((ref.shape[0] // 3,) + ref.shape[1:], ref.dtype)

    for reached, target in ((has_before, before), (has_after, after)):

        @pl.when(reached)
        def _(target=target):
            pl.semaphore_signal(
                barrier, inc=1, device_id=place(target), device_id_type=pl.DeviceIdType.MESH
            )

    pl.semaphore_wait(
        barrier,
        levels + sum(reached.astype(jnp.int32) for reached in (has_prev, has_next, has_before, has_after)),
    )
    point_copies = window_copies(pts, 0)
    start_window(point_copies)

    def load_source(panel):
        row = order[0, panel]
        return field[row], weight[pl.ds(row, 1), :]

    def store_source(panel, values):
        win[panels + panel] = values

    small[2].wait()
    small[3].wait()
    loop(panels, load_source, lambda x, w: (x * w).astype(jnp.bfloat16), store_source, 8)

    chunk = panels // levels

    def window_piece(third_from, third_to, piece, base, target):
        return pltpu.make_async_remote_copy(
            src_ref=win.at[pl.ds(third_from * panels + piece * chunk, chunk)],
            dst_ref=win.at[pl.ds(third_to * panels + piece * chunk, chunk)],
            send_sem=send_sem.at[base + piece],
            recv_sem=recv_sem.at[base + piece],
            device_id=place(target),
            device_id_type=pl.DeviceIdType.MESH,
        )

    direct = [
        window_piece(1, 2 * odd, piece, 4 + levels, device + 1 - 2 * odd)
        for piece in range(levels)
    ]
    passed = [
        window_piece(2 - 2 * odd, 2 * odd, piece, 4 + 2 * levels, pass_to)
        for piece in range(levels)
    ]
    for copy in direct:
        copy.start()

    lane = lax.broadcasted_iota(jnp.int32, (half_rows, rank2), 1)
    low_lanes = lane < rank
    sign = jnp.where(low_lanes, -1.0, 1.0)

    def fold(product):
        return product[:half_rows] + sign * pltpu.roll(product[half_rows:], rank, 1)

    loads[0].wait()

    def matmul(left, right):
        return jnp.dot(left, right, preferred_element_type=jnp.float32)

    def store_compressed(panel, values):
        coeffs[0, panel] = values

    loop(
        panels,
        lambda panel: (win[panels + panel], compress[panel]),
        lambda x, w: fold(matmul(x, w)).astype(jnp.bfloat16),
        store_compressed,
        16,
    )

    def level_copy(level):
        return pltpu.make_async_remote_copy(
            src_ref=coeffs.at[level, pl.ds((1 - bits[level]) * half, half)],
            dst_ref=landed.at[level],
            send_sem=send_sem.at[4 + level],
            recv_sem=recv_sem.at[4 + level],
            device_id=partners[level],
            device_id_type=pl.DeviceIdType.MESH,
        )

    level_copies = [level_copy(0)]
    level_copies[0].start()

    ones = jnp.ones((panels, width), jnp.float32)

    def source_features(window):
        xyz = third(pts, window)[...].astype(jnp.float32)
        square = jnp.full((panels, width), softening * softening, jnp.float32)
        stack = []
        for axis in range(3):
            x = xyz[axis * panels : (axis + 1) * panels]
            square = square + x * x
            stack += [x] * 3
        stack += pieces(square * (PER_TURN * PER_TURN)) + [ones] * 3 + [ones * 0.0]
        for row, values in enumerate(stack):
            src_feat[pl.ds(window * panels, panels), row, :] = values

    def target_features():
        xyz = third(pts, 1)[...].astype(jnp.float32)
        square = jnp.zeros((panels, width), jnp.float32)
        stack = []
        for axis in range(3):
            x = xyz[axis * panels : (axis + 1) * panels]
            square = square + x * x
            stack += pieces(x * (-2.0 * PER_TURN * PER_TURN))
        stack += [ones] * 3 + pieces(square * (PER_TURN * PER_TURN)) + [ones * 0.0]
        for row, values in enumerate(stack):
            tgt_feat[:, row, :] = values

    for load in small[4:]:
        load.wait()
    sort_pairs(
        order_vec[...],
        near_target[pl.ds(device, 1), :],
        near_source[pl.ds(device, 1), :],
        near_count[device],
        ids_vec,
    )
    ids_copy = pltpu.make_async_copy(ids_vec, ids, load_sem.at[2 + levels])
    ids_copy.start()
    target_features()
    source_features(1)
    ids_copy.wait()
    wait_window(point_copies, pts)
    source_features(0)
    source_features(2)

    def load_points(pair):
        return src_feat[ids[0, pair]], tgt_feat[ids[1, pair]]

    def make_tile(source, target):
        squared = lax.dot_general(
            source.astype(jnp.bfloat16),
            target.astype(jnp.bfloat16),
            (((0,), (0,)), ((), ())),
            preferred_element_type=jnp.float32,
        )
        inverse = lax.rsqrt(squared)
        turns = squared * inverse
        part = turns - jnp.round(turns)
        square = part * part
        half_sin = part * poly(square, [math.sqrt(2.0 * AMPLITUDE) * c for c in SIN])
        half_cos = poly(square, [math.sqrt(2.0 * AMPLITUDE) * c for c in COS])
        scaled = inverse * half_sin
        real = AMPLITUDE * inverse - scaled * half_sin
        return real.astype(jnp.bfloat16), (scaled * half_cos).astype(jnp.bfloat16)

    share = pairs // levels

    def mix_level(level):
        bit = bits[level]

        def load_slot(index):
            weights = [mixing[level, index, side] for side in range(2)]
            return (coeffs[level, bit * half + index], landed[level, index], *weights)

        def mix_slot(kept, other, *weights):
            kept, other = kept.astype(jnp.float32), other.astype(jnp.float32)
            low = jnp.where(bit == 1, other, kept)
            high = jnp.where(bit == 1, kept, other)
            real = jnp.where(low_lanes, low, pltpu.roll(high, rank, 1))
            imag = jnp.where(low_lanes, pltpu.roll(low, rank, 1), high)
            stacked = jnp.concatenate([real, imag], 0).astype(jnp.bfloat16)
            return [fold(matmul(stacked, w)).astype(jnp.bfloat16) for w in weights]

        def store_slot(index, values):
            for side in range(2):
                coeffs[level + 1, side * half + index] = values[side]

        loop(half, load_slot, mix_slot, store_slot, 24)

    for level in range(levels):
        first = level * share
        last = pairs if level == levels - 1 else first + share

        def store_tile(pair, values, first=first):
            tiles[first + pair, :, :width] = values[0]
            tiles[first + pair, :, width:] = values[1]

        loop(
            last - first,
            lambda pair, first=first: load_points(first + pair),
            make_tile,
            store_tile,
            6,
        )
        direct[level].wait_recv()

        @pl.when(passes)
        def _(level=level):
            passed[level].start()

        loads[2 + level].wait()
        level_copies[level].wait()
        mix_level(level)
        if level + 1 < levels:
            level_copies.append(level_copy(level + 1))
            level_copies[level + 1].start()

    loads[1].wait()

    def expand_panel(values, weights):
        values = values.astype(jnp.float32)
        stacked = jnp.concatenate([values, pltpu.roll(values, rank, 1)], 0)[:, :rank]
        return matmul(stacked.astype(jnp.bfloat16), weights)

    def store_far(panel, values):
        far[panel] = values

    loop(
        panels,
        lambda panel: (coeffs[levels, panel], expand[panel]),
        expand_panel,
        store_far,
        16,
    )

    for copy in direct:
        copy.wait_send()

    @pl.when(passes)
    def _():
        for copy in passed:
            copy.wait_send()

    @pl.when(gets)
    def _():
        for copy in passed:
            copy.wait_recv()

    @pl.when(jnp.logical_not(gets))
    def _():
        win[pl.ds(2 * odd * panels, panels)] = jnp.zeros((panels, rows, width), win.dtype)

    running[0] = jnp.zeros(running.shape[1:], jnp.float32)
    group_size = math.gcd(pairs, 16)

    def sum_pairs(index, total):
        numbers = [index * group_size + inner for inner in range(group_size)]
        products = [matmul(win[ids[0, pair]], tiles[pair]) for pair in numbers]
        for pair, product in zip(numbers, products):
            total = total * ids[2, pair].astype(jnp.float32) + product
            running[1 + pair] = total
        return total

    lax.fori_loop(
        0, pairs // group_size, sum_pairs, jnp.zeros(running.shape[1:], jnp.float32)
    )

    def write_panel(panel, total):
        out[panel, :half_rows] = total[:half_rows, :width] - total[half_rows:, width:]
        out[panel, half_rows:] = total[:half_rows, width:] + total[half_rows:, :width]

    out_chunk = panels // levels
    out_copies = []
    for piece in range(levels):
        first = piece * out_chunk
        loop(
            out_chunk,
            lambda panel, first=first: (far[ids[3, first + panel]], running[ids[4, first + panel]]),
            lambda x, y: x + y,
            lambda panel, total, first=first: write_panel(first + panel, total),
            6,
        )
        out_copies.append(
            pltpu.make_async_copy(
                out.at[pl.ds(first, out_chunk)],
                out_hbm.at[pl.ds(first, out_chunk)],
                load_sem.at[11 + levels + piece],
            )
        )
        out_copies[-1].start()
    for copy in out_copies:
        copy.wait()


def sort_pairs(order, target, source, count, ids_vec):
    panels, pairs = order.shape[1], target.shape[1]

    def square(size, axis):
        return lax.broadcasted_iota(jnp.int32, (size, size), axis)

    def column(row, size):
        picked = jnp.where(square(size, 0) == square(size, 1), row, 0)
        return jnp.sum(picked, 1, keepdims=True)

    number = lax.broadcasted_iota(jnp.int32, (1, pairs), 1)
    target = jnp.where(number < count, target, panels)
    key = target * pairs + number
    key_col, target_col = column(key, pairs), column(target, pairs)
    source_col = column(source, pairs)
    rank = jnp.sum((key < key_col).astype(jnp.int32), 1, keepdims=True)

    def picked(shift, values):
        hit = rank == square(pairs, 1) - shift
        return jnp.sum(jnp.where(hit, values, 0), 0, keepdims=True)

    by_target = picked(0, target_col)
    ids_vec[0:1, :] = picked(0, source_col)
    ids_vec[1:2, :] = jnp.minimum(by_target, panels - 1)
    ids_vec[2:3, :] = (by_target == picked(1, target_col)).astype(jnp.int32)
    order_col = column(order, panels)
    inverse = jnp.sum(
        jnp.where(order_col == square(panels, 1), square(panels, 0), 0), 0, keepdims=True
    )
    inverse = jnp.minimum(inverse, panels - 1)
    up_to = jnp.sum((target_col <= inverse).astype(jnp.int32), 0, keepdims=True)
    own = jnp.sum((target_col == inverse).astype(jnp.int32), 0, keepdims=True)
    ids_vec[3:4, :panels] = inverse
    ids_vec[4:5, :panels] = jnp.where(own > 0, up_to, 0)


def on_device(
    surface_field,
    positions,
    quad_weight,
    octree_order,
    near_target,
    near_source,
    near_count,
    compress,
    expand,
    mixing,
):
    panels, _, rhs, width = surface_field.shape
    levels, half = mixing.shape[:2]
    pairs = near_target.shape[1]
    rank2 = compress.shape[2]
    spread = lax.axis_size("pan")
    devices = spread * lax.axis_size("grp")
    rows = 2 * rhs
    hbm = pl.BlockSpec(memory_space=pl.ANY)
    result = pl.pallas_call(
        functools.partial(kernel, pairs=pairs, spread=spread, devices=devices),
        out_shape=jax.ShapeDtypeStruct((panels, rows, width), jnp.float32),
        in_specs=[hbm] * 10,
        out_specs=hbm,
        scratch_shapes=[
            pltpu.SMEM(octree_order.shape, jnp.int32),
            pltpu.VMEM(octree_order.shape, jnp.int32),
            pltpu.VMEM(near_target.shape, jnp.int32),
            pltpu.VMEM(near_source.shape, jnp.int32),
            pltpu.SMEM(near_count.shape, jnp.int32),
            pltpu.VMEM((panels, rows, width), jnp.float32),
            pltpu.VMEM(quad_weight.shape, jnp.float32),
            pltpu.VMEM((3 * panels, width), jnp.bfloat16),
            pltpu.VMEM((panels, rows, width), jnp.float32),
            pltpu.VMEM(compress.shape, jnp.bfloat16),
            pltpu.VMEM(expand.shape, jnp.bfloat16),
            pltpu.VMEM((levels, half, 2, rank2, rank2), jnp.bfloat16),
            pltpu.VMEM((3 * panels, rows, width), jnp.bfloat16),
            pltpu.VMEM((3 * panels, width), jnp.float32),
            pltpu.VMEM((3 * panels, width), jnp.float32),
            pltpu.VMEM((9 * panels, width), jnp.bfloat16),
            pltpu.VMEM((3 * panels, FEATURES, width), jnp.float32),
            pltpu.VMEM((panels, FEATURES, width), jnp.float32),
            pltpu.VMEM((pairs, width, 2 * width), jnp.bfloat16),
            pltpu.VMEM((levels + 1, panels, rhs, rank2), jnp.bfloat16),
            pltpu.VMEM((levels, half, rhs, rank2), jnp.bfloat16),
            pltpu.VMEM((panels, rows, 2 * width), jnp.float32),
            pltpu.VMEM((pairs + 1, rows, 2 * width), jnp.float32),
            pltpu.VMEM((8, pairs), jnp.int32),
            pltpu.SMEM((8, pairs), jnp.int32),
            pltpu.SemaphoreType.DMA((11 + 2 * levels,)),
            pltpu.SemaphoreType.DMA((4 + 3 * levels,)),
            pltpu.SemaphoreType.DMA((4 + 3 * levels,)),
        ],
        compiler_params=pltpu.CompilerParams(
            collective_id=0, has_side_effects=True, vmem_limit_bytes=56 * 1024 * 1024
        ),
    )(
        octree_order,
        near_target,
        near_source,
        near_count,
        surface_field.reshape(panels, rows, width),
        quad_weight,
        positions.transpose(1, 0, 2).reshape(3 * panels, width),
        compress,
        expand,
        mixing.reshape(levels, half, 2, rank2, rank2),
    )
    return result.reshape(panels, 2, rhs, width)


def solution(mesh):
    placed = (
        P(("parts", "grp", "pan"), None, None, None),
        P(("parts", "grp", "pan"), None, None),
        P(("parts", "grp", "pan"), None),
        P(("parts", "grp", "pan"), None),
        P("parts", None),
        P("parts", None),
        P("parts"),
        P(("parts", "grp", "pan"), None, None),
        P(("parts", "grp", "pan"), None, None),
        P(None, ("parts", "grp", "pan"), None, None, None, None),
    )
    return jax.shard_map(
        on_device,
        mesh=mesh,
        in_specs=placed,
        out_specs=P(("parts", "grp", "pan"), None, None, None),
        check_vma=False,
    )
```
